32 devices in a mesh: groups: 1, ctx: 4 (over y, x), ep: 8 (over z, core).
Axes of the slice: x: 2, y: 2, z: 4, core: 2. Of those that a mesh axis runs over, the one named last changes fastest.
Arguments:
- query: bfloat16 [8, 256, 4096], P(('groups', 'ep'), 'ctx'), may hold values from -120 to 120
- keys: bfloat16 [8, 256, 256], P(('groups', 'ep'), 'ctx'), may hold values from -6 to 6
- values: bfloat16 [8, 256, 256], P(('groups', 'ep'), 'ctx'), may hold values from -6 to 6
- kept_pos: int32 [8, 256], P(('groups', 'ep'), 'ctx'), may hold values from 0 to 1020, as said below
- hidden: bfloat16 [4096, 2048], P(('groups', 'ctx', 'ep')), may hold values from -6 to 6
- norm_gain: float32 [2048], replicated, may hold values from 0.1 to 1.9
- routes: int32 [4096, 4], P(('groups', 'ctx', 'ep')), may hold values from 0 to 7, all different within a row; in each aligned block of 128 rows (0 to 127, 128 to 255, ...) at most 80 rows name the same one
- route_weight: float32 [4096, 4], P(('groups', 'ctx', 'ep')), may hold values from 0.2 to 1
- capacity: int32 [8], replicated, may hold values from 40 to 80, as said below
- w_gate: bfloat16 [8, 2048, 768], P('ep', 'ctx'), may hold values from -0.125 to 0.125
- w_up: bfloat16 [8, 2048, 768], P('ep', 'ctx'), may hold values from -0.125 to 0.125
- w_down: bfloat16 [8, 768, 2048], P('ep', 'ctx'), may hold values from -0.21875 to 0.21875
Outputs:
- attended: bfloat16 [8, 256, 4096], P(('groups', 'ep'), 'ctx')
- mixed: bfloat16 [4096, 2048], P(('groups', 'ctx', 'ep'))
The draws below stay inside these ranges and needn't reach their ends.
Inputs may be any that keep to these rules, and one draw needn't show every extreme that they name: `kept_pos`: positions are all different within a sequence; every sequence has position 0 and position 1020. `routes`: in the rows of one device no expert is named more than 80 times. `capacity`: some expert has exactly 80.
All inputs are finite; a program needn't handle non-finite values.
Results may differ from the reference program's by a relative error of at most 0.0055.
Values may be sent and summed in bfloat16 or wider, within the bound.
A program may use at most 64 MiB of HBM per device.

```python
import math
import jax
import jax.numpy as jnp
import numpy as np
from jax import lax

D = 2048
HEADS = 32
KVH = 2
HD = 128
FF = 768
TOPK = 4
R = 64
TOK = 128
SEQ = 256
EXPERTS = 8
TOKENS = 4096
CAP = 80
N_EP = 8


def attention_pairs(key):
    second_key = jax.random.fold_in(key, 1)
    base = jnp.clip(jax.random.normal(second_key, (N_EP, SEQ, KVH * HD), jnp.float32), -4.5, 4.5)
    return base


def draw_keys(key, part):
    base = attention_pairs(key)
    result = base
    return result.astype(jnp.bfloat16)


def draw_query(key, part):
    key = jax.random.fold_in(key, 5)
    result = jnp.clip(jax.random.normal(key, (N_EP, SEQ, HEADS * HD), jnp.float32), -4.5, 4.5)
    return result.astype(jnp.bfloat16)


def draw_kept_pos(key, part):
    key = jax.random.fold_in(key, 7)
    first_key, second_key = jax.random.split(key)
    gaps = jax.random.randint(first_key, (N_EP, SEQ), 1, 5)
    positions = jnp.cumsum(gaps, axis=1) - gaps[:, :1]
    positions = positions.at[:, SEQ - 1].set(4 * SEQ - 4)
    half_rows = R // 2
    block_count = SEQ // half_rows
    orders = jax.vmap(lambda sub_key: jax.random.permutation(sub_key, block_count))(jax.random.split(second_key, N_EP))
    blocks = positions.reshape(N_EP, block_count, half_rows)
    placed = jnp.take_along_axis(blocks, orders[:, :, None], axis=1)
    return placed.reshape(N_EP, SEQ).astype(jnp.int32)


def draw_capacity(key, part):
    key = jax.random.fold_in(key, 9)
    first_key, second_key = jax.random.split(key)
    drawn = jax.random.randint(first_key, (EXPERTS,), (CAP + 1) // 2, CAP + 1)
    full_one = jax.random.randint(second_key, (), 0, EXPERTS)
    return jnp.where(jnp.arange(EXPERTS) == full_one, CAP, drawn).astype(jnp.int32)


def block_levels(own_key, dims, cuts, least, top_value):
    level, own = 1.0, jax.random.fold_in(own_key, 6)
    for axis_at, shards_of in cuts:
        draws = jnp.exp(jax.random.uniform(jax.random.fold_in(own, axis_at), (shards_of,), jnp.float32, least / len(cuts), top_value / len(cuts)))
        level = level * jnp.repeat(draws, dims[axis_at] // shards_of).reshape([-1 if axis == axis_at else 1 for axis in range(len(dims))])
    return level


def deal_out(own_key, own, number, rows, amount, top, limit, slope):
    ranking = jax.random.permutation(own_key, amount)
    crowded, ordinary = shares(amount, rows * top, limit, slope, True), shares(amount, rows * top, limit, slope, False)
    places = jnp.arange(amount)

    def named(sizes, turn):
        used = int((sizes > 0).sum())
        fixed = max(1, used // 4)
        moved = fixed + (places - fixed + turn * (used - fixed)) % max(1, amount - fixed)
        return jnp.zeros((amount,), jnp.int32).at[ranking[jnp.where(places < fixed, places, moved)]].set(jnp.asarray(sizes, jnp.int32))

    sizes = jnp.where(number % 4 == 0, named(crowded, number // 4), named(ordinary, number - number // 4 - 1))
    mixed = jax.random.permutation(jax.random.fold_in(own, 3), amount)
    source_of, sink = mixed[0:amount // 2 * 2:2], mixed[1:amount // 2 * 2:2]
    room = jnp.minimum(sizes[source_of] - 1, limit - sizes[sink]) // 2
    room = jnp.where((source_of == ranking[0]) | (sink == ranking[0]) | (sizes[sink] == 0), 0, jnp.maximum(room, 0))
    moved = jax.random.randint(jax.random.fold_in(own, 4), (amount // 2,), 0, 1 << 20) % (room + 1)
    sizes = sizes.at[source_of].add(-moved).at[sink].add(moved)
    items = jnp.searchsorted(jnp.cumsum(sizes), jnp.arange(rows * top), side="right").astype(jnp.int32)
    grid = items.reshape(top, rows).T
    grid = grid[jax.random.permutation(jax.random.fold_in(own, 1), rows)]
    turn = jax.random.randint(jax.random.fold_in(own, 2), (rows, 1), 0, top)
    return jnp.take_along_axis(grid, (jnp.arange(top)[None, :] + turn) % top, axis=1)


def shares(number_of, total, limit, skew, full):
    loads = [(1 << 20) // math.isqrt(rank ** skew) + 1 for rank in range(1, number_of + 1)]
    largest = limit if full else min(limit, max(-(-total // number_of), total * loads[0] // sum(loads)))
    least = 1 if total - largest >= number_of - 1 else 0
    given, rest = [largest] + [least] * (number_of - 1), total - largest - least * (number_of - 1)
    while rest > 0:
        candidates = [i for i in range(1, number_of) if given[i] < largest] or [i for i in range(1, number_of) if given[i] < limit]
        whole, remaining = sum([loads[i] for i in candidates]), rest
        for i in candidates:
            extra = min(limit - given[i], max(1, remaining * loads[i] // whole), rest)
            given[i] = given[i] + extra
            rest = rest - extra
    return np.array(given)


def scatter_about(key, dims, width, most, pieces=(), kind=jnp.bfloat16):
    values = width * jax.random.normal(key, dims, jnp.float32)
    if pieces:
        values = values * block_levels(key, dims, pieces, -0.22, 0.18)
    return jnp.clip(values, -most, most).astype(kind)


def setup_inputs(seed: int = 0, part: int = 0) -> dict:
    streams_of = jax.random.split(jax.random.key(seed), 13)
    part_splits = jax.random.split(jax.random.fold_in(streams_of[12], part), 13)
    query = draw_query(jax.random.fold_in(jax.random.fold_in(streams_of[12], part), 71), part)
    keys = draw_keys(jax.random.fold_in(jax.random.fold_in(streams_of[12], part), 71), part)
    values = scatter_about(part_splits[2], (N_EP, SEQ, KVH * HD), 1.0, 6.0, ((0, 8), (1, 4)))
    kept_pos = draw_kept_pos(jax.random.fold_in(jax.random.fold_in(streams_of[12], part), 71), part)
    hidden = scatter_about(part_splits[4], (TOKENS, D), 1.0, 6.0, ((0, 32),))
    norm_gain = jnp.clip(1.0 + 0.18 * jax.random.normal(streams_of[5], (D,), jnp.float32), 0.1, 1.9)
    routes_keys = jax.random.split(jax.random.fold_in(part_splits[6], 1), TOKENS // TOK)
    routes_turns = jax.random.permutation(jax.random.fold_in(part_splits[6], 3), TOKENS // TOK)
    routes = jax.vmap(lambda own, number: deal_out(jax.random.fold_in(part_splits[6], 2), own, number, TOK, EXPERTS, TOPK, CAP, 2))(routes_keys, routes_turns).reshape((TOKENS, TOPK))
    route_weight = jnp.clip(0.2 + 0.8 * jax.random.uniform(part_splits[7], (TOKENS, TOPK), jnp.float32) ** block_levels(part_splits[7], (TOKENS, TOPK), ((0, 32),), -0.2, 0.2), 0.2, 1.0)
    capacity = draw_capacity(jax.random.fold_in(streams_of[12], 71), part)
    w_gate = scatter_about(streams_of[9], (EXPERTS, D, FF), D ** -0.5, 0.125, ((0, 8), (1, 4)))
    w_up = scatter_about(streams_of[10], (EXPERTS, D, FF), D ** -0.5, 0.125, ((0, 8), (1, 4)))
    w_down = scatter_about(streams_of[11], (EXPERTS, FF, D), FF ** -0.5, 0.21875, ((0, 8), (1, 4)))
    return dict(query=query, keys=keys, values=values, kept_pos=kept_pos, hidden=hidden, norm_gain=norm_gain, routes=routes, route_weight=route_weight, capacity=capacity, w_gate=w_gate, w_up=w_up, w_down=w_down)


def reference(query, keys, values, kept_pos, hidden, norm_gain, routes, route_weight, capacity, w_gate, w_up, w_down):
    group_size = HEADS // KVH
    score_scale = 1.0 / math.sqrt(HD)

    def one_sequence(item_args):
        query_rows, key_rows, value_rows, positions = item_args
        query_heads = query_rows.reshape(SEQ, KVH, group_size, HD).astype(jnp.float32)
        key_heads = key_rows.reshape(SEQ, KVH, HD).astype(jnp.float32)
        value_heads = value_rows.reshape(SEQ, KVH, HD).astype(jnp.float32)
        scores = jnp.einsum('qkgd,skd->kgqs', query_heads, key_heads) * score_scale
        visible = positions[None, :] <= positions[:, None]
        scores = jnp.where(visible[None, None], scores, -jnp.inf)
        row_max = lax.optimization_barrier(jnp.max(scores, axis=-1, keepdims=True))
        probs = jnp.exp(scores - row_max)
        row_total = lax.optimization_barrier(jnp.sum(probs, axis=-1))
        rounded = lax.optimization_barrier(probs.astype(jnp.bfloat16)).astype(jnp.float32)
        summed = jnp.einsum('kgqs,skd->qkgd', rounded, value_heads)
        result = summed / jnp.transpose(row_total, (2, 0, 1))[..., None]
        return result.reshape(SEQ, HEADS * HD).astype(jnp.bfloat16)
    attended = lax.map(one_sequence, (query, keys, values, kept_pos))
    residual = hidden.astype(jnp.float32)
    normed = (residual * lax.rsqrt(lax.optimization_barrier(jnp.mean(residual * residual, axis=-1, keepdims=True)) + 1e-06) * norm_gain).astype(jnp.bfloat16)
    blocks = TOKENS // TOK
    flat_ids = routes.reshape(blocks, TOK * TOPK).astype(jnp.int32)
    onehot = (flat_ids[..., None] == jnp.arange(EXPERTS, dtype=jnp.int32)[None, None, :]).astype(jnp.int32)
    rank_of = lax.optimization_barrier(jnp.sum((jnp.cumsum(onehot, axis=1) - onehot) * onehot, axis=-1))
    kept_mask = rank_of < capacity[flat_ids]
    slot_of = jnp.where(kept_mask, flat_ids * CAP + rank_of, EXPERTS * CAP).astype(jnp.int32)
    token_ids = jnp.broadcast_to(jnp.arange(TOKENS, dtype=jnp.int32).reshape(blocks, TOK, 1), (blocks, TOK, TOPK)).reshape(blocks, TOK * TOPK)
    block_ids = jnp.broadcast_to(jnp.arange(blocks, dtype=jnp.int32)[:, None], (blocks, TOK * TOPK))
    table = jnp.full((blocks, EXPERTS * CAP), -1, jnp.int32).at[block_ids, slot_of].set(token_ids, mode='drop')
    weight_table = jnp.zeros((blocks, EXPERTS * CAP), jnp.float32).at[block_ids, slot_of].set(route_weight.reshape(blocks, TOK * TOPK), mode='drop')
    table = table.reshape(blocks, EXPERTS, CAP).transpose(1, 0, 2).reshape(EXPERTS, blocks * CAP)
    weight_table = weight_table.reshape(blocks, EXPERTS, CAP).transpose(1, 0, 2).reshape(EXPERTS, blocks * CAP)

    def one_expert(carry, expert_item):
        index_rows, weight_rows, gate_mat, up_mat, down_mat = expert_item
        live = index_rows >= 0
        safe_index = jnp.maximum(index_rows, 0)
        expert_rows = jnp.where(live[:, None], normed[safe_index], jnp.zeros((), jnp.bfloat16))
        gate = jnp.dot(expert_rows, gate_mat, preferred_element_type=jnp.float32)
        up_part = jnp.dot(expert_rows, up_mat, preferred_element_type=jnp.float32)
        act = (jax.nn.silu(gate) * up_part).astype(jnp.bfloat16)
        expert_out = jnp.dot(act, down_mat, preferred_element_type=jnp.float32).astype(jnp.bfloat16)
        expert_out = lax.optimization_barrier(expert_out).astype(jnp.float32)
        carry = carry.at[safe_index].add(jnp.where(live[:, None], weight_rows[:, None] * expert_out, jnp.float32(0.0)))
        return (carry, None)
    combined, _ = lax.scan(one_expert, jnp.zeros((TOKENS, D), jnp.float32), (table, weight_table, w_gate, w_up, w_down))
    mixed = (residual + combined).astype(jnp.bfloat16)
    return (attended, mixed)
```

```python
import functools
import math

import jax
import jax.numpy as jnp
from jax import lax
from jax.experimental import pallas as pl
from jax.experimental.pallas import tpu as pltpu
from jax.sharding import PartitionSpec as P

HEADS = 32
KVH = 2
HD = 128
STACK = 4
CHUNKS = 4
F32 = jnp.float32
BF16 = jnp.bfloat16


def kernel(
    n_ctx, n_ep, slots,
    q_ref, k_ref, v_ref, prow_ref, pcol_ref, hid_ref, gain_ref, rt_ref, wt_ref, cap_ref,
    wg_ref, wu_ref, wd_ref,
    att_ref, mix_ref,
    kb, vb, pb, tok, rb, xb, wgb, wub, wdb, gb, ab, yb, sib, ret, own,
    kv_s, kv_r, w_s, w_r, f_s, t_s, t_r, u_s, u_r, s_s, s_r, r_s, r_r,
):
    gi = lax.axis_index("groups")
    c = lax.axis_index("ctx")
    p = lax.axis_index("ep")
    n_z = n_ep // 2
    z, core = p // 2, p % 2
    sibling = z * 2 + (1 - core)
    square = n_ctx == 4
    rows = k_ref.shape[0]
    toks, width = hid_ref.shape
    experts = cap_ref.shape[0]
    ff = wg_ref.shape[1]
    cw = width // CHUNKS

    def dev(cc, pp):
        return (gi, cc, pp)

    barrier = pltpu.get_barrier_semaphore()
    for d in range(1, n_ctx):
        pl.semaphore_signal(barrier, inc=1, device_id=dev(lax.rem(c + d, n_ctx), p), device_id_type=pl.DeviceIdType.MESH)
    for d in range(1, n_z):
        pl.semaphore_signal(barrier, inc=1, device_id=dev(c, lax.rem(z + d, n_z) * 2 + core), device_id_type=pl.DeviceIdType.MESH)
    pl.semaphore_signal(barrier, inc=1, device_id=dev(c, sibling), device_id_type=pl.DeviceIdType.MESH)
    pl.semaphore_wait(barrier, n_ctx + n_z - 1)

    def copy(src, dst, ss, rs, to):
        return pltpu.make_async_remote_copy(
            src_ref=src, dst_ref=dst, send_sem=ss, recv_sem=rs,
            device_id=to, device_id_type=pl.DeviceIdType.MESH)

    if square:
        cx = c + 1 - 2 * (c % 2)
        cy = lax.rem(c + 2, 4)
        cd = 3 - c
        direct = [cx, cy]
        others = [cx, cy, cd]
    else:
        direct = [lax.rem(c + d, n_ctx) for d in range(1, n_ctx)]
        others = direct
    pending = []

    kb[pl.ds(pl.multiple_of(c * rows, rows), rows), :] = k_ref[...]
    vb[pl.ds(pl.multiple_of(c * rows, rows), rows), :] = v_ref[...]
    pb[c] = prow_ref[...]

    def kv_copies(i, src, to):
        at = pl.ds(pl.multiple_of(src * rows, rows), rows)
        return [
            copy(kb.at[at], kb.at[at], kv_s.at[i, 0], kv_r.at[src, 0], to),
            copy(vb.at[at], vb.at[at], kv_s.at[i, 1], kv_r.at[src, 1], to),
            copy(pb.at[src], pb.at[src], kv_s.at[i, 2], kv_r.at[src, 2], to),
        ]

    for i, cc in enumerate(others):
        for cp in kv_copies(i, c, dev(cc, p)):
            cp.start()
            pending.append(cp)

    def piece(i, src, half):
        if i < 2:
            ref, buf = (wg_ref, wgb) if i == 0 else (wu_ref, wub)
            n = ref.shape[0]
            cols = pl.ds(0, ff)
        else:
            ref, buf = wd_ref, wdb
            n = ref.shape[0]
            cols = pl.ds((i - 2) * cw, cw)
        h = n // 2
        there = buf.at[pl.ds(pl.multiple_of(src * n + half * h, h), h), cols]
        return ref.at[pl.ds(half * h, h), cols], there

    def send_own(i):
        for order in range(2):
            for k, cc in enumerate(direct):
                half = order if k % 2 == 0 else 1 - order
                here, there = piece(i, c, half)
                cp = copy(here, there, w_s.at[i, k, half], w_r.at[i, c, half], dev(cc, p))
                cp.start()
                pending.append(cp)

    def arrived(i, src, half):
        _, there = piece(i, src, half)
        copy(there, there, w_s.at[i, 0, half], w_r.at[i, src, half], dev(direct[0], p)).wait_recv()

    def pass_on(i):
        if square:
            for src, half, to in ((cx, 0, cy), (cy, 1, cx)):
                arrived(i, src, half)
                _, there = piece(i, src, half)
                cp = copy(there, there, f_s.at[i, half], w_r.at[i, src, half], dev(to, p))
                cp.start()
                pending.append(cp)

    def finish(i):
        if square:
            for src, half in ((cx, 1), (cy, 0), (cd, 0), (cd, 1)):
                arrived(i, src, half)
        else:
            for src in direct:
                for half in range(2):
                    arrived(i, src, half)

    send_own(0)

    hid = hid_ref[...].astype(F32)
    scale = lax.rsqrt(jnp.mean(hid * hid, axis=-1, keepdims=True) + 1e-06)
    tok[z, core] = (hid * scale * gain_ref[...]).astype(BF16)
    eid = lax.broadcasted_iota(jnp.int32, (experts, toks), 0)
    named = jnp.zeros((experts, toks), F32)
    share = jnp.zeros((experts, toks), F32)
    for k in range(rt_ref.shape[0]):
        hit = rt_ref[k : k + 1, :] == eid
        named = jnp.where(hit, 1.0, named)
        share = jnp.where(hit, wt_ref[k : k + 1, :], share)
    before = (
        lax.broadcasted_iota(jnp.int32, (toks, toks), 0)
        < lax.broadcasted_iota(jnp.int32, (toks, toks), 1)
    ).astype(F32).astype(BF16)
    rank = jnp.dot(named.astype(BF16), before, preferred_element_type=F32)
    kept = (named > 0.5) & (rank < cap_ref[...].astype(F32))
    rb[z, core, :experts, :] = jnp.where(kept, rank, -1.0)
    rb[z, core, experts:, :] = jnp.where(kept, share, 0.0)

    def tok_copies(zz, cc, ss, rs, to):
        return (
            copy(tok.at[zz, cc], tok.at[zz, cc], ss.at[0], rs.at[0], to),
            copy(rb.at[zz, cc], rb.at[zz, cc], ss.at[1], rs.at[1], to),
        )

    def z_copies(d):
        to = dev(c, lax.rem(z + d, n_z) * 2 + core)
        return tok_copies(z, core, t_s.at[d], t_r.at[z], to)

    def z_arrivals(zz):
        return tok_copies(zz, core, t_s.at[0], t_r.at[zz], dev(c, sibling))

    def sib_copies(zz):
        return tok_copies(zz, core, u_s.at[zz], u_r.at[zz], dev(c, sibling))

    def sib_arrivals(zz):
        return tok_copies(zz, 1 - core, u_s.at[zz], u_r.at[zz], dev(c, sibling))

    @pl.loop(1, n_z)
    def _(d):
        for cp in z_copies(d):
            cp.start()

    for cp in sib_copies(z):
        cp.start()
    send_own(1)

    for src in others:
        for cp in kv_copies(0, src, dev(direct[0], p)):
            cp.wait_recv()
    key_pos = jnp.sum(pb[...], axis=0)[0:1, :]
    visible = key_pos <= pcol_ref[:, 0:1]
    bias = jnp.where(visible, 0.0, -jnp.inf)
    bias = jnp.concatenate([bias] * STACK, axis=0)
    per = HEADS // KVH
    for h0 in range(0, HEADS, STACK):
        g = h0 // per
        qs = jnp.concatenate([q_ref[:, (h0 + s) * HD : (h0 + s + 1) * HD] for s in range(STACK)], axis=0)
        sc = lax.dot_general(qs, kb[:, g * HD : (g + 1) * HD], (((1,), (1,)), ((), ())), preferred_element_type=F32)
        sc = sc * (1.0 / math.sqrt(HD)) + bias
        pr = jnp.exp(sc - jnp.max(sc, axis=-1, keepdims=True))
        total = jnp.sum(pr, axis=-1, keepdims=True)
        o = jnp.dot(pr.astype(BF16), vb[:, g * HD : (g + 1) * HD], preferred_element_type=F32) / total
        o = o.astype(BF16)
        for s in range(STACK):
            att_ref[:, (h0 + s) * HD : (h0 + s + 1) * HD] = o[s * rows : (s + 1) * rows]

    pass_on(0)

    def keep(ref, buf):
        n = ref.shape[0]
        buf[pl.ds(pl.multiple_of(c * n, n), n), :] = ref[...]

    keep(wg_ref, wgb)
    keep(wu_ref, wub)
    keep(wd_ref, wdb)
    pass_on(1)
    for i in range(CHUNKS):
        send_own(2 + i)

    slot_id = lax.broadcasted_iota(jnp.int32, (slots, toks), 0).astype(F32)

    def dispatch(zz, cc):
        hot = (rb[zz, cc, pl.ds(p, 1), :] == slot_id).astype(F32).astype(BF16)
        at = pl.ds(pl.multiple_of((zz * 2 + cc) * slots, slots), slots)
        xb[at, :] = jnp.dot(hot, tok[zz, cc], preferred_element_type=F32).astype(BF16)

    dispatch(z, core)

    @pl.loop(1, n_z)
    def _(d):
        zz = lax.rem(z + d, n_z)
        for cp in z_arrivals(zz):
            cp.wait_recv()
        for cp in sib_copies(zz):
            cp.start()
        dispatch(zz, core)

    @pl.loop(0, n_z)
    def _(d):
        zz = lax.rem(z + d, n_z)
        for cp in sib_arrivals(zz):
            cp.wait_recv()
        dispatch(zz, 1 - core)

    @pl.loop(1, n_z)
    def _(d):
        for cp in z_copies(d):
            cp.wait_send()

    @pl.loop(0, n_z)
    def _(d):
        for cp in sib_copies(d):
            cp.wait_send()

    ft = 256

    finish(0)

    @pl.loop(0, ff // ft)
    def _(t):
        at = pl.ds(pl.multiple_of(t * ft, ft), ft)
        gate = jnp.dot(xb[...], wgb[:, at], preferred_element_type=F32)
        gb[:, at] = gate / (1.0 + jnp.exp(-gate))

    finish(1)

    @pl.loop(0, ff // ft)
    def _(t):
        at = pl.ds(pl.multiple_of(t * ft, ft), ft)
        up = jnp.dot(xb[...], wub[:, at], preferred_element_type=F32)
        ab[:, at] = (gb[:, at] * up).astype(BF16)

    def combined(zz, cc):
        live = rb[zz, cc, pl.ds(p, 1), :] == slot_id
        weight = jnp.where(live, rb[zz, cc, pl.ds(experts + p, 1), :], 0.0)
        high = weight.astype(BF16)
        low = (weight - high.astype(F32)).astype(BF16)
        at = pl.ds(pl.multiple_of((zz * 2 + cc) * slots, slots), slots)
        y = yb[at, :]
        dims = (((0,), (0,)), ((), ()))
        return lax.dot_general(high, y, dims, preferred_element_type=F32) + lax.dot_general(
            low, y, dims, preferred_element_type=F32
        )

    def ret_copy(j, d):
        zz = lax.rem(z + d, n_z)
        cols = pl.ds(j * cw, cw)
        return copy(tok.at[zz, core, :, cols], ret.at[z, :, cols], r_s.at[j, d], r_r.at[j, z], dev(c, zz * 2 + core))

    def ret_arrival(j, d):
        zz = lax.rem(z + d, n_z)
        cols = pl.ds(j * cw, cw)
        return copy(tok.at[zz, core, :, cols], ret.at[zz, :, cols], r_s.at[j, d], r_r.at[j, zz], dev(c, zz * 2 + core))

    for j in range(CHUNKS):
        cols = pl.ds(j * cw, cw)
        pass_on(2 + j)
        finish(2 + j)
        for t in range(0, cw, ft):
            yb[:, t : t + ft] = jnp.dot(
                ab[...], wdb[:, j * cw + t : j * cw + t + ft], preferred_element_type=F32
            ).astype(BF16)

        @pl.loop(0, n_z)
        def _(zz):
            tok[zz, 1 - core, :, cols] = combined(zz, 1 - core).astype(BF16)

        pair = copy(tok.at[:, 1 - core, :, cols], sib.at[:, :, cols], s_s.at[j], s_r.at[j], dev(c, sibling))
        pair.start()
        pending.append(pair)
        own[:, cols] = combined(z, core)
        pair.wait_recv()

        @pl.loop(1, n_z)
        def _(d):
            zz = lax.rem(z + d, n_z)
            tok[zz, core, :, cols] = (combined(zz, core) + sib[zz, :, cols].astype(F32)).astype(BF16)
            ret_copy(j, d).start()

        own[:, cols] += sib[z, :, cols].astype(F32)

    for j in range(CHUNKS):
        cols = pl.ds(j * cw, cw)

        @pl.loop(1, n_z)
        def _(d):
            ret_arrival(j, d).wait_recv()
            own[:, cols] += ret[lax.rem(z + d, n_z), :, cols].astype(F32)

        mix_ref[:, cols] = (hid_ref[:, cols].astype(F32) + own[:, cols]).astype(BF16)

    for cp in pending:
        cp.wait_send()
    for j in range(CHUNKS):

        @pl.loop(1, n_z)
        def _(d):
            ret_copy(j, d).wait_send()


def body(query, keys, values, kept_pos, hidden, norm_gain, routes, route_weight, capacity, w_gate, w_up, w_down, n_ctx, n_ep):
    rows = query.shape[1]
    toks, width = hidden.shape
    topk = routes.shape[1]
    experts = capacity.shape[0]
    assert w_gate.shape[0] == 1
    cap = min(toks, max(2, 5 * toks * topk // (4 * experts)))
    slots = -(-cap // 16) * 16
    ff = w_gate.shape[2]
    n_z = n_ep // 2
    pieces = 2 + CHUNKS
    c = lax.axis_index("ctx")
    pos = kept_pos[0].astype(F32)
    lane = jnp.arange(n_ctx * rows) // rows
    prow = jnp.broadcast_to(jnp.where(lane == c, jnp.tile(pos, n_ctx), 0.0)[None], (8, n_ctx * rows))
    pcol = jnp.broadcast_to(pos[:, None], (rows, 128))
    capb = jnp.broadcast_to(capacity[:, None], (experts, toks))
    dma = pltpu.SemaphoreType.DMA
    vm = pl.BlockSpec(memory_space=pltpu.VMEM)
    attended, mixed = pl.pallas_call(
        functools.partial(kernel, n_ctx, n_ep, slots),
        out_shape=(
            jax.ShapeDtypeStruct((rows, query.shape[2]), BF16),
            jax.ShapeDtypeStruct((toks, width), BF16),
        ),
        in_specs=[vm] * 13,
        out_specs=(vm, vm),
        scratch_shapes=[
            pltpu.VMEM((n_ctx * rows, KVH * HD), BF16),
            pltpu.VMEM((n_ctx * rows, KVH * HD), BF16),
            pltpu.VMEM((n_ctx, 8, n_ctx * rows), F32),
            pltpu.VMEM((n_z, 2, toks, width), BF16),
            pltpu.VMEM((n_z, 2, 2 * experts, toks), F32),
            pltpu.VMEM((n_ep * slots, width), BF16),
            pltpu.VMEM((width, ff), BF16),
            pltpu.VMEM((width, ff), BF16),
            pltpu.VMEM((ff, width), BF16),
            pltpu.VMEM((n_ep * slots, ff), F32),
            pltpu.VMEM((n_ep * slots, ff), BF16),
            pltpu.VMEM((n_ep * slots, width // CHUNKS), BF16),
            pltpu.VMEM((n_z, toks, width), BF16),
            pltpu.VMEM((n_z, toks, width), BF16),
            pltpu.VMEM((toks, width), F32),
            dma((n_ctx, 3)),
            dma((n_ctx, 3)),
            dma((pieces, n_ctx, 2)),
            dma((pieces, n_ctx, 2)),
            dma((pieces, 2)),
            dma((n_z, 2)),
            dma((n_z, 2)),
            dma((n_z, 2)),
            dma((n_z, 2)),
            dma((CHUNKS,)),
            dma((CHUNKS,)),
            dma((CHUNKS, n_z)),
            dma((CHUNKS, n_z)),
        ],
        compiler_params=pltpu.CompilerParams(
            collective_id=0, has_side_effects=True, vmem_limit_bytes=62 * 1024 * 1024
        ),
    )(
        query[0], keys[0], values[0], prow, pcol, hidden, norm_gain[None], routes.T, route_weight.T, capb,
        w_gate[0], w_up[0], w_down[0],
    )
    return attended[None], mixed


def solution(mesh):
    placed = (
        P(("groups", "ep"), "ctx", None),
        P(("groups", "ep"), "ctx", None),
        P(("groups", "ep"), "ctx", None),
        P(("groups", "ep"), "ctx"),
        P(("groups", "ctx", "ep"), None),
        P(),
        P(("groups", "ctx", "ep"), None),
        P(("groups", "ctx", "ep"), None),
        P(),
        P("ep", "ctx", None),
        P("ep", "ctx", None),
        P("ep", "ctx", None),
    )
    return jax.shard_map(
        functools.partial(body, n_ctx=mesh.shape["ctx"], n_ep=mesh.shape["ep"]),
        mesh=mesh,
        in_specs=placed,
        out_specs=(P(("groups", "ep"), "ctx", None), P(("groups", "ctx", "ep"), None)),
        check_vma=False,
    )
```

```python
import functools
import math

import jax
import jax.numpy as jnp
from jax import lax
from jax.experimental import pallas as pl
from jax.experimental.pallas import tpu as pltpu
from jax.sharding import PartitionSpec as P

HEADS = 32
KVH = 2
HD = 128
STACK = 4
CHUNKS = 4
F32 = jnp.float32
BF16 = jnp.bfloat16


def kernel(
    n_ctx, n_ep, slots,
    q_ref, k_ref, v_ref, pos_ref, hid_ref, gain_ref, rt_ref, wt_ref, cap_ref,
    wg_ref, wu_ref, wd_ref,
    att_ref, mix_ref,
    kb, vb, pb, tok, rb, xb, wgb, wub, wdb, gb, ab, yb, sib, ret, own, comb, rel,
    kv_s, kv_r, w_s, w_r, f_s, t_s, t_r, u_s, u_r, s_s, s_r, r_s, r_r, l_s, x_s, x_r,
):
    gi = lax.axis_index("groups")
    c = lax.axis_index("ctx")
    p = lax.axis_index("ep")
    n_z = n_ep // 2
    z, core = p // 2, p % 2
    sibling = z * 2 + (1 - core)
    square = n_ctx == 4
    rows = k_ref.shape[0]
    toks, width = hid_ref.shape
    experts = cap_ref.shape[1]
    ff = wg_ref.shape[1]
    cw = width // CHUNKS

    def dev(cc, pp):
        return (gi, cc, pp)

    barrier = pltpu.get_barrier_semaphore()
    for d in range(1, n_ctx):
        pl.semaphore_signal(barrier, inc=1, device_id=dev(lax.rem(c + d, n_ctx), p), device_id_type=pl.DeviceIdType.MESH)
    for d in range(1, n_z):
        pl.semaphore_signal(barrier, inc=1, device_id=dev(c, lax.rem(z + d, n_z) * 2 + core), device_id_type=pl.DeviceIdType.MESH)
    pl.semaphore_signal(barrier, inc=1, device_id=dev(c, sibling), device_id_type=pl.DeviceIdType.MESH)
    pl.semaphore_wait(barrier, n_ctx + n_z - 1)

    def copy(src, dst, ss, rs, to):
        return pltpu.make_async_remote_copy(
            src_ref=src, dst_ref=dst, send_sem=ss, recv_sem=rs,
            device_id=to, device_id_type=pl.DeviceIdType.MESH)

    if square:
        cx = c + 1 - 2 * (c % 2)
        cy = lax.rem(c + 2, 4)
        cd = 3 - c
        direct = [cx, cy]
        others = [cx, cy, cd]
    else:
        direct = [lax.rem(c + d, n_ctx) for d in range(1, n_ctx)]
        others = direct
    pending = []

    kb[pl.ds(pl.multiple_of(c * rows, rows), rows), :] = k_ref[...]
    vb[pl.ds(pl.multiple_of(c * rows, rows), rows), :] = v_ref[...]
    pos = pos_ref[...].astype(F32)
    every = jnp.concatenate([pos] * n_ctx, axis=1)
    lane = lax.broadcasted_iota(jnp.int32, (8, n_ctx * rows), 1)
    pb[c] = jnp.where((lane >= c * rows) & (lane < (c + 1) * rows), every, 0.0)

    def column(row):
        n = row.shape[1]
        diag = lax.broadcasted_iota(jnp.int32, (n, n), 0) == lax.broadcasted_iota(jnp.int32, (n, n), 1)
        return jnp.sum(jnp.where(diag, row, 0.0), axis=1, keepdims=True)

    def kv_copies(i, src, to):
        at = pl.ds(pl.multiple_of(src * rows, rows), rows)
        return [
            copy(kb.at[at], kb.at[at], kv_s.at[i, 0], kv_r.at[src, 0], to),
            copy(vb.at[at], vb.at[at], kv_s.at[i, 1], kv_r.at[src, 1], to),
            copy(pb.at[src], pb.at[src], kv_s.at[i, 2], kv_r.at[src, 2], to),
        ]

    for i, cc in enumerate(others):
        for cp in kv_copies(i, c, dev(cc, p)):
            cp.start()
            pending.append(cp)

    def piece(i, src, half):
        if i < 2:
            ref, buf = (wg_ref, wgb) if i == 0 else (wu_ref, wub)
            n = ref.shape[0]
            cols = pl.ds(0, ff)
        else:
            ref, buf = wd_ref, wdb
            n = ref.shape[0]
            cols = pl.ds((i - 2) * cw, cw)
        h = n // 2
        there = buf.at[pl.ds(pl.multiple_of(src * n + half * h, h), h), cols]
        return ref.at[pl.ds(half * h, h), cols], there

    def send_own(i):
        for order in range(2):
            for k, cc in enumerate(direct):
                half = order if k % 2 == 0 else 1 - order
                here, there = piece(i, c, half)
                cp = copy(here, there, w_s.at[i, k, half], w_r.at[i, c, half], dev(cc, p))
                cp.start()
                pending.append(cp)

    def arrived(i, src, half):
        _, there = piece(i, src, half)
        copy(there, there, w_s.at[i, 0, half], w_r.at[i, src, half], dev(direct[0], p)).wait_recv()

    def pass_on(i):
        if square:
            for src, half, to in ((cx, 0, cy), (cy, 1, cx)):
                arrived(i, src, half)
                _, there = piece(i, src, half)
                cp = copy(there, there, f_s.at[i, half], w_r.at[i, src, half], dev(to, p))
                cp.start()
                pending.append(cp)

    def finish(i):
        if square:
            for src, half in ((cx, 1), (cy, 0), (cd, 0), (cd, 1)):
                arrived(i, src, half)
        else:
            for src in direct:
                for half in range(2):
                    arrived(i, src, half)

    def keep(i, ref, buf):
        n = ref.shape[0]
        return pltpu.make_async_copy(ref, buf.at[pl.ds(pl.multiple_of(c * n, n), n)], l_s.at[i])

    local = [keep(0, wg_ref, wgb), keep(1, wu_ref, wub), keep(2, wd_ref, wdb)]
    send_own(0)
    for cp in local:
        cp.start()

    hid = hid_ref[...].astype(F32)
    scale = lax.rsqrt(jnp.mean(hid * hid, axis=-1, keepdims=True) + 1e-06)
    tok[z, core] = (hid * scale * gain_ref[...]).astype(BF16)
    eid = lax.broadcasted_iota(jnp.int32, (experts, toks), 0)
    named = jnp.zeros((experts, toks), F32)
    share = jnp.zeros((experts, toks), F32)
    for k in range(rt_ref.shape[0]):
        hit = rt_ref[k : k + 1, :] == eid
        named = jnp.where(hit, 1.0, named)
        share = jnp.where(hit, wt_ref[k : k + 1, :], share)
    before = (
        lax.broadcasted_iota(jnp.int32, (toks, toks), 0)
        < lax.broadcasted_iota(jnp.int32, (toks, toks), 1)
    ).astype(F32).astype(BF16)
    rank = jnp.dot(named.astype(BF16), before, preferred_element_type=F32)
    kept = (named > 0.5) & (rank < column(cap_ref[...].astype(F32)))
    rb[z, core, :experts, :] = jnp.where(kept, rank, -1.0)
    rb[z, core, experts:, :] = jnp.where(kept, share, 0.0)

    def tok_copies(zz, cc, ss, rs, to):
        return (
            copy(tok.at[zz, cc], tok.at[zz, cc], ss.at[0], rs.at[0], to),
            copy(rb.at[zz, cc], rb.at[zz, cc], ss.at[1], rs.at[1], to),
        )

    def z_copies(d):
        to = dev(c, lax.rem(z + d, n_z) * 2 + core)
        return tok_copies(z, core, t_s.at[d], t_r.at[z], to)

    def z_arrivals(zz):
        return tok_copies(zz, core, t_s.at[0], t_r.at[zz], dev(c, sibling))

    def sib_copies(zz):
        return tok_copies(zz, core, u_s.at[zz], u_r.at[zz], dev(c, sibling))

    def sib_arrivals(zz):
        return tok_copies(zz, 1 - core, u_s.at[zz], u_r.at[zz], dev(c, sibling))

    @pl.loop(1, n_z)
    def _(d):
        for cp in z_copies(d):
            cp.start()

    for cp in sib_copies(z):
        cp.start()
    send_own(1)

    for src in others:
        for cp in kv_copies(0, src, dev(direct[0], p)):
            cp.wait_recv()
    key_pos = jnp.sum(pb[...], axis=0)[0:1, :]
    visible = key_pos <= column(pos)
    bias = jnp.where(visible, 0.0, -jnp.inf)
    bias = jnp.concatenate([bias] * STACK, axis=0)
    per = HEADS // KVH
    for h0 in range(0, HEADS, STACK):
        g = h0 // per
        qs = jnp.concatenate([q_ref[:, (h0 + s) * HD : (h0 + s + 1) * HD] for s in range(STACK)], axis=0)
        sc = lax.dot_general(qs, kb[:, g * HD : (g + 1) * HD], (((1,), (1,)), ((), ())), preferred_element_type=F32)
        sc = sc * (1.0 / math.sqrt(HD)) + bias
        pr = jnp.exp(sc - jnp.max(sc, axis=-1, keepdims=True))
        total = jnp.sum(pr, axis=-1, keepdims=True)
        o = jnp.dot(pr.astype(BF16), vb[:, g * HD : (g + 1) * HD], preferred_element_type=F32) / total
        o = o.astype(BF16)
        for s in range(STACK):
            att_ref[:, (h0 + s) * HD : (h0 + s + 1) * HD] = o[s * rows : (s + 1) * rows]

    pass_on(0)

    pass_on(1)

    slot_id = lax.broadcasted_iota(jnp.int32, (slots, toks), 0).astype(F32)

    def dispatch(zz, cc):
        hot = (rb[zz, cc, pl.ds(p, 1), :] == slot_id).astype(F32).astype(BF16)
        at = pl.ds(pl.multiple_of((zz * 2 + cc) * slots, slots), slots)
        xb[at, :] = jnp.dot(hot, tok[zz, cc], preferred_element_type=F32).astype(BF16)
        weight = jnp.where(rb[zz, cc, pl.ds(p, 1), :] == slot_id, rb[zz, cc, pl.ds(experts + p, 1), :], 0.0)
        comb[zz, cc] = weight.T.astype(BF16)

    dispatch(z, core)

    @pl.loop(1, n_z)
    def _(d):
        zz = lax.rem(z + d, n_z)
        for cp in z_arrivals(zz):
            cp.wait_recv()
        for cp in sib_copies(zz):
            cp.start()
        dispatch(zz, core)

    @pl.loop(0, n_z)
    def _(d):
        zz = lax.rem(z + d, n_z)
        for cp in sib_arrivals(zz):
            cp.wait_recv()
        dispatch(zz, 1 - core)

    @pl.loop(1, n_z)
    def _(d):
        for cp in z_copies(d):
            cp.wait_send()

    @pl.loop(0, n_z)
    def _(d):
        for cp in sib_copies(d):
            cp.wait_send()

    ft = 256

    for cp in local:
        cp.wait()
    finish(0)
    send_own(2)

    @pl.loop(0, ff // ft)
    def _(t):
        at = pl.ds(pl.multiple_of(t * ft, ft), ft)
        gate = jnp.dot(xb[...], wgb[:, at], preferred_element_type=F32)
        gb[:, at] = gate / (1.0 + jnp.exp(-gate))

    finish(1)
    for j in range(1, min(3, CHUNKS)):
        send_own(2 + j)

    @pl.loop(0, ff // ft)
    def _(t):
        at = pl.ds(pl.multiple_of(t * ft, ft), ft)
        up = jnp.dot(xb[...], wub[:, at], preferred_element_type=F32)
        ab[:, at] = (gb[:, at] * up).astype(BF16)

    def combined(zz, cc):
        at = pl.ds(pl.multiple_of((zz * 2 + cc) * slots, slots), slots)
        return jnp.dot(comb[zz, cc], yb[at, :], preferred_element_type=F32)

    line = n_z == 4
    low = z == 0
    high = z == 3
    end = low | high
    if line:
        first = jnp.where(low, 2, jnp.where(high, 1, z - 1))
        second = jnp.where(low, 1, jnp.where(high, 2, z + 1))
        far = jnp.where(z < 2, 3, 0)
        inner = jnp.where(z < 2, 1, 2)

    def ret_copy(j, zz):
        cols = pl.ds(j * cw, cw)
        return copy(tok.at[zz, core, :, cols], ret.at[z, :, cols], r_s.at[j, zz], r_r.at[j, z], dev(c, zz * 2 + core))

    def ret_arrival(j, zz):
        cols = pl.ds(j * cw, cw)
        return copy(tok.at[zz, core, :, cols], ret.at[zz, :, cols], r_s.at[j, zz], r_r.at[j, zz], dev(c, zz * 2 + core))

    def relay(j):
        cols = pl.ds(j * cw, cw)
        return copy(tok.at[far, core, :, cols], rel.at[:, cols], x_s.at[j], x_r.at[j], dev(c, inner * 2 + core))

    def part(j, zz):
        return combined(zz, core) + sib[zz, :, j * cw : (j + 1) * cw].astype(F32)

    pass_on(2)
    for j in range(CHUNKS):
        cols = pl.ds(j * cw, cw)
        finish(2 + j)
        for t in range(0, cw, ft):
            yb[:, t : t + ft] = jnp.dot(
                ab[...], wdb[:, j * cw + t : j * cw + t + ft], preferred_element_type=F32
            ).astype(BF16)

        @pl.loop(0, n_z)
        def _(zz):
            tok[zz, 1 - core, :, cols] = combined(zz, 1 - core).astype(BF16)

        pair = copy(tok.at[:, 1 - core, :, cols], sib.at[:, :, cols], s_s.at[j], s_r.at[j], dev(c, sibling))
        pair.start()
        pending.append(pair)
        if j + 3 < CHUNKS:
            send_own(2 + j + 3)
        own[:, cols] = combined(z, core)
        pair.wait_recv()
        if line:

            @pl.when(end)
            def _():
                tok[far, core, :, cols] = part(j, far).astype(BF16)
                relay(j).start()

            for zz in (first, second):
                tok[zz, core, :, cols] = part(j, zz).astype(BF16)
                ret_copy(j, zz).start()

            @pl.when(jnp.logical_not(end))
            def _():
                mine = part(j, far)
                relay(j).wait_recv()
                tok[far, core, :, cols] = (mine + rel[:, cols].astype(F32)).astype(BF16)
                ret_copy(j, far).start()

        else:

            @pl.loop(1, n_z)
            def _(d):
                zz = lax.rem(z + d, n_z)
                tok[zz, core, :, cols] = part(j, zz).astype(BF16)
                ret_copy(j, zz).start()

        own[:, cols] += sib[z, :, cols].astype(F32)
        if j + 1 < CHUNKS:
            pass_on(2 + j + 1)

    for j in range(CHUNKS):
        cols = pl.ds(j * cw, cw)

        def take(zz):
            ret_arrival(j, zz).wait_recv()
            own[:, cols] += ret[zz, :, cols].astype(F32)

        if line:
            for zz in (first, second):
                take(jnp.where(end, 3 - zz, zz))

            @pl.when(jnp.logical_not(end))
            def _():
                take(far)

        else:

            @pl.loop(1, n_z)
            def _(d):
                take(lax.rem(z + d, n_z))

        mix_ref[:, cols] = (hid_ref[:, cols].astype(F32) + own[:, cols]).astype(BF16)

    for cp in pending:
        cp.wait_send()
    for j in range(CHUNKS):
        if line:
            for zz in (first, second):
                ret_copy(j, zz).wait_send()

            @pl.when(end)
            def _():
                relay(j).wait_send()

            @pl.when(jnp.logical_not(end))
            def _():
                ret_copy(j, far).wait_send()

        else:

            @pl.loop(1, n_z)
            def _(d):
                ret_copy(j, lax.rem(z + d, n_z)).wait_send()


def body(query, keys, values, kept_pos, hidden, norm_gain, routes, route_weight, capacity, w_gate, w_up, w_down, n_ctx, n_ep):
    rows = query.shape[1]
    toks, width = hidden.shape
    topk = routes.shape[1]
    experts = capacity.shape[0]
    assert w_gate.shape[0] == 1
    cap = min(toks, max(2, 5 * toks * topk // (4 * experts)))
    slots = -(-cap // 16) * 16
    ff = w_gate.shape[2]
    n_z = n_ep // 2
    pieces = 2 + CHUNKS
    dma = pltpu.SemaphoreType.DMA
    vm = pl.BlockSpec(memory_space=pltpu.VMEM)
    attended, mixed = pl.pallas_call(
        functools.partial(kernel, n_ctx, n_ep, slots),
        out_shape=(
            jax.ShapeDtypeStruct((rows, query.shape[2]), BF16),
            jax.ShapeDtypeStruct((toks, width), BF16),
        ),
        in_specs=[vm] * 9 + [pl.BlockSpec(memory_space=pl.ANY)] * 3,
        out_specs=(vm, vm),
        scratch_shapes=[
            pltpu.VMEM((n_ctx * rows, KVH * HD), BF16),
            pltpu.VMEM((n_ctx * rows, KVH * HD), BF16),
            pltpu.VMEM((n_ctx, 8, n_ctx * rows), F32),
            pltpu.VMEM((n_z, 2, toks, width), BF16),
            pltpu.VMEM((n_z, 2, 2 * experts, toks), F32),
            pltpu.VMEM((n_ep * slots, width), BF16),
            pltpu.VMEM((width, ff), BF16),
            pltpu.VMEM((width, ff), BF16),
            pltpu.VMEM((ff, width), BF16),
            pltpu.VMEM((n_ep * slots, ff), F32),
            pltpu.VMEM((n_ep * slots, ff), BF16),
            pltpu.VMEM((n_ep * slots, width // CHUNKS), BF16),
            pltpu.VMEM((n_z, toks, width), BF16),
            pltpu.VMEM((n_z, toks, width), BF16),
            pltpu.VMEM((toks, width), F32),
            pltpu.VMEM((n_z, 2, toks, slots), BF16),
            pltpu.VMEM((toks, width), BF16),
            dma((n_ctx, 3)),
            dma((n_ctx, 3)),
            dma((pieces, n_ctx, 2)),
            dma((pieces, n_ctx, 2)),
            dma((pieces, 2)),
            dma((n_z, 2)),
            dma((n_z, 2)),
            dma((n_z, 2)),
            dma((n_z, 2)),
            dma((CHUNKS,)),
            dma((CHUNKS,)),
            dma((CHUNKS, n_z)),
            dma((CHUNKS, n_z)),
            dma((3,)),
            dma((CHUNKS,)),
            dma((CHUNKS,)),
        ],
        compiler_params=pltpu.CompilerParams(
            collective_id=0, has_side_effects=True, vmem_limit_bytes=62 * 1024 * 1024
        ),
    )(
        query[0], keys[0], values[0], kept_pos, hidden, norm_gain[None], routes.T, route_weight.T, capacity[None],
        w_gate[0], w_up[0], w_down[0],
    )
    return attended[None], mixed


def solution(mesh):
    placed = (
        P(("groups", "ep"), "ctx", None),
        P(("groups", "ep"), "ctx", None),
        P(("groups", "ep"), "ctx", None),
        P(("groups", "ep"), "ctx"),
        P(("groups", "ctx", "ep"), None),
        P(),
        P(("groups", "ctx", "ep"), None),
        P(("groups", "ctx", "ep"), None),
        P(),
        P("ep", "ctx", None),
        P("ep", "ctx", None),
        P("ep", "ctx", None),
    )
    return jax.shard_map(
        functools.partial(body, n_ctx=mesh.shape["ctx"], n_ep=mesh.shape["ep"]),
        mesh=mesh,
        in_specs=placed,
        out_specs=(P(("groups", "ep"), "ctx", None), P(("groups", "ctx", "ep"), None)),
        check_vma=False,
    )
```
